32 devices in a mesh: dp: 2 (over core), expert: 16 (over z, y, x).
Axes of the slice: x: 2, y: 2, z: 4, core: 2. Of those that a mesh axis runs over, the one named last changes fastest.
Arguments:
- tokens: bfloat16 [4096, 4096], P(('dp', 'expert')), parts along dimension 0, may hold values from -6 to 6
- w_gate_up: bfloat16 [16, 2, 4096, 768], P('expert'), may hold values from -0.09375 to 0.09375
- w_down: bfloat16 [16, 768, 4096], P('expert'), may hold values from -0.21875 to 0.21875
- routes: int32 [4096, 8], P(('dp', 'expert')), parts along dimension 0, may hold values from 0 to 15, as said below
- gate_scaled: int32 [4096, 8], P(('dp', 'expert')), parts along dimension 0, may hold values from 1 to 1023
Outputs:
- mixed: bfloat16 [4096, 4096], P(('dp', 'expert')), parts along dimension 0
The draws below stay inside these ranges and needn't reach their ends.
There are 2 independent parts, one for each index of `dp`. The reference program is written for one: setup_inputs(seed, part) draws one part's arguments, and reference() takes and returns one part's arrays. A program takes and returns all parts, laid end to end along the dimension named above; an argument that names none is the same for every part. Nothing has to cross between parts.
Inputs may be any that keep to these rules, and one draw needn't show every extreme that they name: `routes`: every row names 8 different experts. In each aligned block of 128 rows (the rows of one device) one expert, the same in every block, is named by exactly 128 rows; no other expert is named by more than 80 rows of a block, and a second expert, the same in every block, by exactly 80 rows of every block.
All inputs are finite; a program needn't handle non-finite values.
Results may differ from the reference program's by a relative error of at most 0.0057.
Values may be sent and summed in bfloat16 or wider, within the bound.
A program may use at most 192 MiB of HBM per device.

```python
import jax
import jax.numpy as jnp
from jax import lax

D = 4096
FFW = 768
TOP = 8
TOK_DEV = 128
EXPERTS = 16
TOKENS = 2048
COLD = 80
MOST = 128
N_EXPERT = 16


def draw_routes(key, part):
    blocks = TOKENS // TOK_DEV
    labels = jax.random.permutation(jax.random.fold_in(key, 11), EXPERTS).astype(jnp.int32)
    remaining = TOK_DEV * TOP - MOST - COLD

    def shuffle_row(row_key):
        return jax.random.permutation(row_key, TOP)

    def one_block(block_index):
        block_key = jax.random.fold_in(key, block_index)
        capacity_units = jax.random.permutation(jax.random.fold_in(block_key, 1), (EXPERTS - 2) * COLD)
        chosen = (capacity_units < remaining).astype(jnp.int32).reshape(EXPERTS - 2, COLD)
        counts = jnp.concatenate([jnp.array([MOST, COLD], jnp.int32), jnp.sum(chosen, axis=1).astype(jnp.int32)])
        listed = jnp.repeat(labels, counts, total_repeat_length=TOK_DEV * TOP)
        assigned = listed.reshape(TOP, TOK_DEV).T
        row_order = jax.random.permutation(jax.random.fold_in(block_key, 2), TOK_DEV)
        assigned = assigned[row_order]
        column_keys = jax.random.split(jax.random.fold_in(block_key, 3), TOK_DEV)
        column_orders = jax.vmap(shuffle_row)(column_keys)
        return jnp.take_along_axis(assigned, column_orders, axis=1)
    return jax.vmap(one_block)(jnp.arange(blocks)).reshape(TOKENS, TOP).astype(jnp.int32)


def plant(values, key, smallest, high):
    index_at = [jax.random.randint(jax.random.fold_in(key, axis), (), 0, length) for axis, length in enumerate(values.shape)]
    widest = values.shape.index(max(values.shape))
    neighbour = index_at[:widest] + [(index_at[widest] + 1) % values.shape[widest]] + index_at[widest + 1:]
    return values.at[tuple(index_at)].set(smallest).at[tuple(neighbour)].set(high)


def block_levels(own_key, extent, shards, smallest, top_value):
    loudness, own = 1.0, jax.random.fold_in(own_key, 6)
    for position, blocks in shards:
        draws = jnp.exp(jax.random.uniform(jax.random.fold_in(own, position), (blocks,), jnp.float32, smallest / len(shards), top_value / len(shards)))
        loudness = loudness * jnp.repeat(draws, extent[position] // blocks).reshape([-1 if axis == position else 1 for axis in range(len(extent))])
    return loudness


def bell_draw(key, dims, scale, bound, cuts=(), held_as=jnp.bfloat16):
    values = jax.random.normal(key, dims, jnp.float32) * scale
    if len(cuts) > 0:
        values = block_levels(key, dims, cuts, -0.22, 0.18) * values
    return jnp.clip(values, min=-bound, max=bound).astype(held_as)


def setup_inputs(seed: int = 0, part: int = 0) -> dict:
    keys = jax.random.split(jax.random.key(seed), 6)
    part_keys = jax.random.split(jax.random.fold_in(keys[5], part), 6)
    return {
        "tokens": bell_draw(part_keys[0], (TOKENS, D), 1.0, 6.0, ((0, 16),)),
        "w_gate_up": bell_draw(keys[1], (EXPERTS, 2, D, FFW), D ** -0.5, 0.09375, ((0, 16),)),
        "w_down": bell_draw(keys[2], (EXPERTS, FFW, D), FFW ** -0.5, 0.21875, ((0, 16),)),
        "routes": draw_routes(jax.random.fold_in(jax.random.fold_in(keys[5], part), 71), part),
        "gate_scaled": plant(jax.random.randint(part_keys[4], (TOKENS, TOP), 1, 1024), jax.random.fold_in(part_keys[4], 1), 1, 1023).astype(jnp.int32),
    }


def expert_rows(picked, gate_up, down_proj):
    gate_val = jnp.dot(picked, gate_up[0], preferred_element_type=jnp.float32)
    up_val = jnp.dot(picked, gate_up[1], preferred_element_type=jnp.float32)
    hidden = (jax.nn.silu(gate_val) * up_val).astype(jnp.bfloat16)
    return jnp.dot(hidden, down_proj, preferred_element_type=jnp.float32).astype(jnp.bfloat16)


def reference(tokens, w_gate_up, w_down, routes, gate_scaled):
    slot_total = TOKENS * TOP
    flat_routes = routes.reshape(-1)
    capacity = N_EXPERT * MOST

    def per_expert(carry, expert):
        indices = jnp.nonzero(flat_routes == expert, size=capacity, fill_value=slot_total)[0].astype(jnp.int32)
        token_index = jnp.minimum(indices // TOP, TOKENS - 1).astype(jnp.int32)
        picked = jnp.take(tokens, token_index, axis=0)
        gate_up = lax.dynamic_index_in_dim(w_gate_up, expert, 0, keepdims=False)
        down_proj = lax.dynamic_index_in_dim(w_down, expert, 0, keepdims=False)
        results = expert_rows(picked, gate_up, down_proj)
        return carry.at[indices].set(results, mode="drop"), None

    filled, _ = lax.scan(per_expert, jnp.zeros((slot_total, D), jnp.bfloat16), jnp.arange(EXPERTS, dtype=jnp.int32))
    scaled = gate_scaled.astype(jnp.float32)
    weight = scaled / jnp.sum(scaled, axis=1, keepdims=True)
    mixed = jnp.einsum("tk,tkd->td", weight, filled.reshape(TOKENS, TOP, D).astype(jnp.float32))
    return mixed.astype(jnp.bfloat16)
```

```python
import jax
import jax.numpy as jnp
from jax import lax
from jax.sharding import PartitionSpec as P

CHUNKS = 2


def expert_rows(picked, gate_up, down_proj):
    gate_val = jnp.dot(picked, gate_up[0], preferred_element_type=jnp.float32)
    up_val = jnp.dot(picked, gate_up[1], preferred_element_type=jnp.float32)
    hidden = (jax.nn.silu(gate_val) * up_val).astype(jnp.bfloat16)
    return jnp.dot(hidden, down_proj, preferred_element_type=jnp.float32).astype(jnp.bfloat16)


def body(tokens, w_gate_up, w_down, routes, gate_scaled):
    experts = lax.axis_size("expert")
    tok_rows, model_width = tokens.shape
    gate_up = w_gate_up[0]
    down_proj = w_down[0]
    scaled = gate_scaled.astype(jnp.float32)
    weight = scaled / jnp.sum(scaled, axis=1, keepdims=True)
    names = jnp.arange(experts, dtype=jnp.int32)[:, None, None]
    share = jnp.sum(jnp.where(routes[None] == names, weight[None], 0.0), axis=2)
    share = lax.all_to_all(share, "expert", split_axis=0, concat_axis=0, tiled=True)
    rows = tok_rows // CHUNKS
    mixed = []
    for chunk in range(CHUNKS):
        part = slice(chunk * rows, (chunk + 1) * rows)
        gathered = lax.all_gather(tokens[part], "expert", axis=0, tiled=True)
        expert_out = expert_rows(gathered, gate_up, down_proj)
        scale = share[:, part].reshape(-1, 1)
        weighted = (scale * expert_out.astype(jnp.float32)).astype(jnp.bfloat16)
        mixed.append(lax.psum_scatter(weighted, "expert", scatter_dimension=0, tiled=True))
    return jnp.concatenate(mixed, axis=0)


def solution(mesh):
    return jax.shard_map(
        body,
        mesh=mesh,
        in_specs=(
            P(("dp", "expert"), None),
            P("expert", None, None, None),
            P("expert", None, None),
            P(("dp", "expert"), None),
            P(("dp", "expert"), None),
        ),
        out_specs=P(("dp", "expert"), None),
        check_vma=False,
    )
```

```python
import jax
import jax.numpy as jnp
from jax import lax
from jax.sharding import PartitionSpec as P

CHUNKS = 2


def hidden_rows(picked, gate_up):
    gate_val = jnp.dot(picked, gate_up[0], preferred_element_type=jnp.float32)
    up_val = jnp.dot(picked, gate_up[1], preferred_element_type=jnp.float32)
    return (jax.nn.silu(gate_val) * up_val).astype(jnp.bfloat16)


def halving_sum(blocks, order):
    experts = blocks.shape[0]
    bits = experts.bit_length() - 1
    me = lax.axis_index("expert")
    data = blocks.reshape((2,) * bits + blocks.shape[1:])
    left = list(range(bits - 1, -1, -1))
    for bit in order:
        axis = left.index(bit)
        left.remove(bit)
        mine = (me >> bit) & 1
        keep = lax.dynamic_index_in_dim(data, mine, axis, keepdims=False)
        send = lax.dynamic_index_in_dim(data, 1 - mine, axis, keepdims=False)
        swap = [(device, device ^ (1 << bit)) for device in range(experts)]
        came = lax.ppermute(send, "expert", swap)
        data = (keep.astype(jnp.float32) + came.astype(jnp.float32)).astype(blocks.dtype)
    return data


def body(tokens, w_gate_up, w_down, routes, gate_scaled):
    experts = lax.axis_size("expert")
    tok_rows, model_width = tokens.shape
    gate_up = w_gate_up[0]
    down_proj = w_down[0]
    scaled = gate_scaled.astype(jnp.float32)
    weight = scaled / jnp.sum(scaled, axis=1, keepdims=True)
    names = jnp.arange(experts, dtype=jnp.int32)[:, None, None]
    share = jnp.sum(jnp.where(routes[None] == names, weight[None], 0.0), axis=2)
    share = lax.all_to_all(share, "expert", split_axis=0, concat_axis=0, tiled=True)
    rows = tok_rows // CHUNKS
    bits = experts.bit_length() - 1
    far = list(range(bits - 1, 1, -1))
    eighth = model_width // 8
    groups = (
        (0, 3 * eighth, [0, 1] + far),
        (3 * eighth, 6 * eighth, [1, 0] + far),
        (6 * eighth, model_width, [2, 0, 1] + far[:-1]),
    )
    mixed = []
    for chunk in range(CHUNKS):
        part = slice(chunk * rows, (chunk + 1) * rows)
        gathered = lax.all_gather(tokens[part], "expert", axis=0, tiled=True)
        hidden = hidden_rows(gathered, gate_up)
        scale = share[:, part].reshape(-1, 1)
        columns = []
        for start, stop, order in groups:
            expert_out = jnp.dot(
                hidden, down_proj[:, start:stop], preferred_element_type=jnp.float32
            ).astype(jnp.bfloat16)
            weighted = (scale * expert_out.astype(jnp.float32)).astype(jnp.bfloat16)
            columns.append(halving_sum(weighted.reshape(experts, rows, stop - start), order))
        mixed.append(jnp.concatenate(columns, axis=1))
    return jnp.concatenate(mixed, axis=0)


def solution(mesh):
    return jax.shard_map(
        body,
        mesh=mesh,
        in_specs=(
            P(("dp", "expert"), None),
            P("expert", None, None, None),
            P("expert", None, None),
            P(("dp", "expert"), None),
            P(("dp", "expert"), None),
        ),
        out_specs=P(("dp", "expert"), None),
        check_vma=False,
    )
```

```python
import jax
import jax.numpy as jnp
from jax import lax
from jax.sharding import PartitionSpec as P

CHUNKS = 2


def hidden_rows(picked, gate_up):
    gate_val = jnp.dot(picked, gate_up[0], preferred_element_type=jnp.float32)
    up_val = jnp.dot(picked, gate_up[1], preferred_element_type=jnp.float32)
    return (jax.nn.silu(gate_val) * up_val).astype(jnp.bfloat16)


def halving_sum(blocks, order):
    experts = blocks.shape[0]
    bits = experts.bit_length() - 1
    me = lax.axis_index("expert")
    data = blocks.reshape((2,) * bits + blocks.shape[1:])
    left = list(range(bits - 1, -1, -1))
    for bit in order:
        axis = left.index(bit)
        left.remove(bit)
        mine = (me >> bit) & 1
        keep = lax.dynamic_index_in_dim(data, mine, axis, keepdims=False)
        send = lax.dynamic_index_in_dim(data, 1 - mine, axis, keepdims=False)
        swap = [(device, device ^ (1 << bit)) for device in range(experts)]
        came = lax.ppermute(send, "expert", swap)
        data = (keep.astype(jnp.float32) + came.astype(jnp.float32)).astype(blocks.dtype)
    return data


def doubling_gather(rows, order):
    experts = lax.axis_size("expert")
    me = lax.axis_index("expert")
    data = rows
    held = []
    for bit in reversed(order):
        swap = [(device, device ^ (1 << bit)) for device in range(experts)]
        came = lax.ppermute(data, "expert", swap)
        first = ((me >> bit) & 1) == 0
        held = sorted(held + [bit], reverse=True)
        pair = [jnp.where(first, data, came), jnp.where(first, came, data)]
        data = jnp.stack(pair, axis=held.index(bit))
    return data.reshape(experts * rows.shape[0], rows.shape[1])


def body(tokens, w_gate_up, w_down, routes, gate_scaled):
    experts = lax.axis_size("expert")
    tok_rows, model_width = tokens.shape
    gate_up = w_gate_up[0]
    down_proj = w_down[0]
    scaled = gate_scaled.astype(jnp.float32)
    weight = scaled / jnp.sum(scaled, axis=1, keepdims=True)
    names = jnp.arange(experts, dtype=jnp.int32)[:, None, None]
    share = jnp.sum(jnp.where(routes[None] == names, weight[None], 0.0), axis=2)
    share = lax.all_to_all(share, "expert", split_axis=0, concat_axis=0, tiled=True)
    rows = tok_rows // CHUNKS
    bits = experts.bit_length() - 1
    far = list(range(bits - 1, 1, -1))
    eighth = model_width // 8
    groups = (
        (0, 3 * eighth, [0, 1] + far),
        (3 * eighth, 6 * eighth, [1, 0] + far),
        (6 * eighth, model_width, [2, 0, 1] + far[:-1]),
    )
    mixed = []
    for chunk in range(CHUNKS):
        part = slice(chunk * rows, (chunk + 1) * rows)
        gathered = jnp.concatenate(
            [doubling_gather(tokens[part, start:stop], order) for start, stop, order in groups], axis=1
        )
        hidden = hidden_rows(gathered, gate_up)
        scale = share[:, part].reshape(-1, 1)
        columns = []
        for start, stop, order in groups:
            expert_out = jnp.dot(
                hidden, down_proj[:, start:stop], preferred_element_type=jnp.float32
            ).astype(jnp.bfloat16)
            weighted = (scale * expert_out.astype(jnp.float32)).astype(jnp.bfloat16)
            columns.append(halving_sum(weighted.reshape(experts, rows, stop - start), order))
        mixed.append(jnp.concatenate(columns, axis=1))
    return jnp.concatenate(mixed, axis=0)


def solution(mesh):
    return jax.shard_map(
        body,
        mesh=mesh,
        in_specs=(
            P(("dp", "expert"), None),
            P("expert", None, None, None),
            P("expert", None, None),
            P(("dp", "expert"), None),
            P(("dp", "expert"), None),
        ),
        out_specs=P(("dp", "expert"), None),
        check_vma=False,
    )
```
